512 devices in a mesh: bin: 2 (over core), row: 16 (over y, x), col: 16 (over z).
Axes of the slice: x: 4, y: 4, z: 16, core: 2. Of those that a mesh axis runs over, the one named last changes fastest.
Arguments:
- gamma: bfloat16 [4, 2, 2048, 2048], P('bin', None, 'row', 'col'), parts along dimension 0, may hold values from -200 to 200, as said below
- right_side: float32 [4, 2, 2048, 2048], P('bin', None, 'row', 'col'), parts along dimension 0, may hold values from -26 to 26
Outputs:
- solution: float32 [4, 2, 2048, 2048], P('bin', None, 'row', 'col'), parts along dimension 0
- residual: float32 [4, 2, 2048, 2048], P('bin', None, 'row', 'col'), parts along dimension 0
The draws below stay inside these ranges and needn't reach their ends.
There are 2 independent parts, one for each index of `bin`. The reference program is written for one: setup_inputs(seed, part) draws one part's arguments, and reference() takes and returns one part's arrays. A program takes and returns all parts, laid end to end along the dimension named above; each array names one. Nothing has to cross between parts.
Inputs may be any that keep to these rules, and one draw needn't show every extreme that they name: Each bin's gamma is Hermitian (gamma[0] symmetric, gamma[1] antisymmetric) and positive definite.
All inputs are finite; a program needn't handle non-finite values.
Results may differ from the reference program's by a relative error of at most 0.011.
Values may be sent and summed in bfloat16 or wider, within the bound.
A program may use at most 64 MiB of HBM per device.

```python
import math
import jax
import jax.numpy as jnp

N = 2048
M = 2048
BINS = 2
ITERS = 3


def station_scales(key, spread):
    key = jax.random.fold_in(key, 11)
    ramp = jnp.arange(N, dtype=jnp.float32) / N
    rough = jax.random.uniform(key, (N,), jnp.float32, 0.0, 1.0)
    return jnp.exp(0.5 * math.log(3.0) * ramp + spread * rough)


def one_gamma(key):
    first_key, second_key, scale_key = jax.random.split(key, 3)
    sigma = 1.0 / math.sqrt(2.0 * N)
    first = jax.random.normal(first_key, (N, N), jnp.float32)
    second = jax.random.normal(second_key, (N, N), jnp.float32)
    spread = 0.5 * math.log(10.0)
    herm_real = (first + first.T) * (sigma / math.sqrt(2.0))
    herm_imag = (second - second.T) * (sigma / math.sqrt(2.0))
    scales = station_scales(scale_key, spread)
    outer = scales[:, None] * scales[None, :]
    real_part = outer * (3.5 * jnp.eye(N, dtype=jnp.float32) + herm_real)
    imag_part = outer * herm_imag
    return jnp.stack([real_part, imag_part])


def draw_gamma(key, part):
    key = jax.random.fold_in(key, 1)
    keys = jax.random.split(key, BINS)
    return jax.vmap(one_gamma)(keys).astype(jnp.bfloat16)


def draw_right_side(key, part):
    key = jax.random.fold_in(key, 2)
    rough = jax.random.normal(key, (BINS, 2, N, M), jnp.float32)
    return 4.0 * jnp.clip(rough, -6.0, 6.0)


def setup_inputs(seed: int = 0, part: int = 0) -> dict:
    key_list = jax.random.split(jax.random.key(seed), 3)
    own_keys = jax.random.split(jax.random.fold_in(key_list[2], part), 3)
    gamma = draw_gamma(jax.random.fold_in(jax.random.fold_in(key_list[2], part), 71), part)
    right_side = draw_right_side(jax.random.fold_in(jax.random.fold_in(key_list[2], part), 71), part)
    return dict(gamma=gamma, right_side=right_side)


EPS_REL = 0.1


def column_sum(first, second):
    return jnp.sum(first[0] * second[0] + first[1] * second[1], axis=0)


def operate(gamma, direction, shift):
    lowered = direction.astype(jnp.bfloat16)
    real_part = jnp.dot(gamma[0], lowered[0], preferred_element_type=jnp.float32) - jnp.dot(gamma[1], lowered[1], preferred_element_type=jnp.float32)
    imag_part = jnp.dot(gamma[0], lowered[1], preferred_element_type=jnp.float32) + jnp.dot(gamma[1], lowered[0], preferred_element_type=jnp.float32)
    return jnp.stack([real_part + shift * direction[0], imag_part + shift * direction[1]])


def solve_bin(gamma, right_side):
    trace_total = jnp.sum(jnp.diagonal(gamma[0]).astype(jnp.float32))
    shift = EPS_REL * trace_total / N
    solution = jnp.zeros_like(right_side)
    residual = right_side
    direction = right_side
    norm_now = column_sum(residual, residual)
    for step in range(ITERS):
        image = operate(gamma, direction, shift)
        alpha = norm_now / column_sum(direction, image)
        solution = solution + alpha * direction
        residual = residual - alpha * image
        if step + 1 < ITERS:
            norm_next = column_sum(residual, residual)
            direction = residual + (norm_next / norm_now) * direction
            norm_now = norm_next
    return solution, residual


def reference(gamma, right_side):
    solutions = []
    residuals = []
    for index in range(BINS):
        solved, left_over = solve_bin(gamma[index], right_side[index])
        solutions.append(solved)
        residuals.append(left_over)
    return jnp.stack(solutions), jnp.stack(residuals)
```

```python
import jax
import jax.numpy as jnp
from jax import lax
from jax.experimental import pallas as pl
from jax.experimental.pallas import tpu as pltpu
from jax.sharding import PartitionSpec as P

MESH = pl.DeviceIdType.MESH
N = 2048
ITERS = 3
EPS_REL = 0.1
T = 128
SB = 8
LANES = 512


def kernel(gamma, rhs, out_s, out_r,
           W, bT, B, X, Xs, Y, Z, shs, dir_, res, sol, img, O, R,
           zr, zs, br, bs, rs, ss, xr, xs, yr, ys, shr_sem, shs_sem, orr, ors):
    h = lax.axis_index("bin")
    i = lax.axis_index("row")
    z = lax.axis_index("col")
    y, x = i // 4, i % 4
    j = z // 4
    hb, bl_me = (z % 4) // 2, z % 2
    big = i // 2
    first_half = y < 2

    def dev(b, r, c):
        return {"bin": b, "row": r, "col": c}

    def is_me(b, r, c):
        return (b == h) & (r == i) & (c == z)

    def step_x(row, d):
        return (row // 4) * 4 + (row % 4 + d) % 4

    def step_y(row, d):
        return (row // 4 + d) % 4 * 4 + row % 4

    barrier = pltpu.get_barrier_semaphore()

    def greet(b, r, c, maybe_me):
        def far():
            pl.semaphore_signal(barrier, inc=1, device_id=dev(b, r, c), device_id_type=MESH)
        if maybe_me:
            pl.when(jnp.logical_not(is_me(b, r, c)))(far)
        else:
            far()

    for k in range(16):
        greet(hb, i, k, True)
    for k in range(16):
        greet(hb, k, 4 * j + x, True)
    for d in (1, 2, 3):
        greet(h, step_x(i, d), z, False)
        greet(h, step_y(i, d), z, False)
    greet(1 - h, i, z, False)

    for bl in range(2):
        for part in range(2):
            tile = rhs[bl, part].T
            for g in range(8):
                bT[bl, g, 16 * part:16 * part + 16, :] = tile[16 * g:16 * g + 16, :]

    mine = jnp.where(h == hb, 1, 0)
    pl.semaphore_wait(barrier, 39 - mine - mine * jnp.where(z % 4 == x, 1, 0))

    def send(src, dst, send_sem, recv_sem, target):
        return pltpu.make_async_remote_copy(
            src_ref=src, dst_ref=dst, send_sem=send_sem, recv_sem=recv_sem,
            device_id=dev(*target), device_id_type=MESH)

    t = (z - 2 * big + 16) % 16
    chosen = (t < 8) | ((t < 10) & (big < 4))

    def tile_copies():
        n = 0
        for bl in range(2):
            for jj in range(4):
                for q in range(2):
                    target = (q, i, 4 * jj + 2 * h + bl)
                    yield is_me(*target), target, gamma.at[bl, q], zs.at[n]
                    n += 1

    @pl.when(chosen)
    def _():
        for me, target, src, sem in tile_copies():
            @pl.when(jnp.logical_not(me))
            def _(src=src, sem=sem, target=target):
                send(src, W.at[i, t], sem, zr.at[t], target).start()
            @pl.when(me)
            def _(src=src):
                pltpu.make_async_copy(src, W.at[i, t], zr.at[t]).start()

    def rhs_copies():
        n = 0
        for bl in range(2):
            for yy in range(4):
                for q in range(2):
                    target = (q, 4 * yy + z % 4, 4 * j + 2 * h + bl)
                    yield is_me(*target), target, bT.at[bl, 2 * yy + q], bs.at[n], B.at[i]
                    n += 1

    for me, target, src, sem, dst in rhs_copies():
        @pl.when(jnp.logical_not(me))
        def _(src=src, sem=sem, dst=dst, target=target):
            send(src, dst, sem, br.at[i], target).start()
        @pl.when(me)
        def _(src=src, dst=dst):
            pltpu.make_async_copy(src, dst, br.at[i]).start()

    sib = (1 - h, i, z)

    def panel(row, d):
        return W.at[row, 2 * d:2 * d + 2]

    def panel_send(row, d, n, target_row):
        return send(panel(row, d), panel(row, d), ss.at[d, n], rs.at[row, d], (h, target_row, z))

    def panel_wait(row, d):
        panel_send(row, d, 0, step_x(i, 1)).wait_recv()

    def axes(d):
        return (step_x, step_y) if d % 2 == 0 else (step_y, step_x)

    def when(cond, body):
        if cond is True:
            body()
        else:
            pl.when(cond)(body)

    def row_ok(d, row):
        return True if d < 4 else row < 8

    def forward_side(d, e):
        return 1 if (d // 2 + e) % 2 == 0 else 3

    def stage_a(d):
        first, second = axes(d)
        def body():
            for u in (2 * d, 2 * d + 1):
                send(gamma.at[0, 0], W.at[i, u], zs.at[0], zr.at[u], sib).wait_recv()
            for n, e in enumerate((1, 3, 2)):
                panel_send(i, d, n, first(i, e)).start()
            for n, e in enumerate((1, 3)):
                panel_send(i, d, 3 + n, second(i, e)).start()
        when(row_ok(d, i), body)

    def stage_b(d):
        first, second = axes(d)
        def body():
            for n, e in enumerate((1, 3, 2)):
                row = first(i, e)
                panel_wait(row, d)
                for m, f in enumerate((1, 3)):
                    panel_send(row, d, 5 + 2 * n + m, second(i, f)).start()
        when(row_ok(d, i), body)

    def stage_c(d):
        first, second = axes(d)
        for side in (1, 3):
            def body(side=side):
                for e in range(4):
                    row = first(second(i, side), e)
                    panel_wait(row, d)
                    if forward_side(d, e) == side:
                        panel_send(row, d, 11 + e, second(i, 4 - side)).start()
            when(row_ok(d, second(i, side)), body)

    def stage_e(d):
        first, second = axes(d)
        def body():
            for e in range(4):
                panel_wait(first(second(i, 2), e), d)
        when(row_ok(d, second(i, 2)), body)

    def rhs_arrived():
        for k in range(16):
            send(bT.at[0, 0], B.at[k], bs.at[0], br.at[k], sib).wait_recv()
        for k in range(16):
            cols = slice(T * k, T * k + T)
            value = B[k]
            X[0, h, k] = value.astype(jnp.bfloat16)
            dir_[:, cols] = value
            res[:, cols] = value
        send(X.at[0, h], X.at[0, h], xs.at[0], xr.at[0], sib).start()
        sol[...] = jnp.zeros_like(sol)

    stage_a(0)
    stage_a(1)
    stage_b(0)
    stage_a(2)
    stage_b(1)
    stage_c(0)
    rhs_arrived()
    stage_a(3)
    stage_b(2)
    stage_c(1)
    stage_a(4)
    stage_b(3)
    stage_c(2)
    stage_b(4)
    stage_c(3)
    stage_c(4)
    for d in range(5):
        stage_e(d)

    total = jnp.zeros((T, T), jnp.float32)
    for k in range(16):
        total = total + W[k, k % 2].astype(jnp.float32)
    eye = lax.broadcasted_iota(jnp.int32, (T, T), 0) == lax.broadcasted_iota(jnp.int32, (T, T), 1)
    total = jnp.where(eye, total, 0.0)
    trace = jnp.sum(jnp.sum(total, axis=0, keepdims=True), axis=1, keepdims=True)
    shs[0] = jnp.broadcast_to(EPS_REL * trace / N, (8, T))
    shift_copy = send(shs.at[0], shs.at[1], shs_sem.at[0], shr_sem.at[0], sib)
    shift_copy.start()

    def both(v):
        s = v[:16] + v[16:]
        return jnp.concatenate([s, s], axis=0)

    def row_sum(parts):
        total = parts[0]
        for p in parts[1:]:
            total = total + p
        return both(jnp.sum(total, axis=1, keepdims=True))

    slabs = [slice(a, a + LANES) for a in range(0, N, LANES)]
    rr0 = row_sum([res[:, s] * res[:, s] for s in slabs])
    shift_copy.wait()
    shift = jnp.where(h == 0, shs[0], shs[1])[:1, :1]

    sign = jnp.where(h == 0, 1.0, -1.0).astype(jnp.bfloat16)

    def super_tile(a, d):
        return jnp.concatenate(
            [jnp.concatenate([W[2 * a, 2 * d], W[2 * a, 2 * d + 1]], axis=1),
             jnp.concatenate([W[2 * a + 1, 2 * d], W[2 * a + 1, 2 * d + 1]], axis=1)], axis=0)

    def x_block(ref_value, a):
        return jnp.concatenate([ref_value(2 * a), ref_value(2 * a + 1)], axis=1)

    def iteration(it, rr):
        send(X.at[it, h], X.at[it, h], xs.at[it], xr.at[it], sib).wait_recv()
        for k in range(16):
            Xs[k] = X[it, :, k].reshape(64, T) * sign

        def plain(k):
            return X[it, :, k].reshape(64, T)

        def signed(k):
            return Xs[k]

        for c in range(SB):
            acc = jnp.zeros((64, 256), jnp.float32)
            for d in range(5):
                a = (c - d) % SB
                if d < 4 or a < 4:
                    acc = acc + jnp.dot(x_block(signed, a), super_tile(a, d), preferred_element_type=jnp.float32)
                if d > 0 and (d < 4 or c < 4):
                    k = (c + d) % SB
                    acc = acc + lax.dot_general(
                        x_block(plain, k), super_tile(c, d), (((1,), (1,)), ((), ())),
                        preferred_element_type=jnp.float32)
            Y[:, :, 256 * c:256 * c + 256] = acc.reshape(2, 32, 256)

        swap = send(Y.at[1 - h], Z.at[it], ys.at[it], yr.at[it], sib)
        swap.start()
        swap.wait()

        curve = []
        for s in slabs:
            own, other = Y[h, :, s], Z[it, :, s]
            real = jnp.where(h == 0, own, other)
            imag = jnp.where(h == 0, other, own)
            d = dir_[:, s]
            image = real + jnp.concatenate([-imag[16:], imag[:16]], axis=0) + shift * d
            img[:, s] = image
            curve.append(d * image)
        alpha = rr / row_sum(curve)
        norm = []
        for s in slabs:
            sol[:, s] = sol[:, s] + alpha * dir_[:, s]
            r = res[:, s] - alpha * img[:, s]
            res[:, s] = r
            norm.append(r * r)
        new = row_sum(norm)

        @pl.when(it + 1 < ITERS)
        def _():
            beta = new / rr
            for k in range(16):
                cols = slice(T * k, T * k + T)
                d = res[:, cols] + beta * dir_[:, cols]
                dir_[:, cols] = d
                X[it + 1, h, k] = d.astype(jnp.bfloat16)
            send(X.at[it + 1, h], X.at[it + 1, h], xs.at[it + 1], xr.at[it + 1], sib).start()

        return new

    lax.fori_loop(0, ITERS, iteration, rr0)

    for k in range(16):
        cols = slice(T * k, T * k + T)
        O[k, 0] = sol[:, cols].astype(jnp.bfloat16)
        O[k, 1] = res[:, cols].astype(jnp.bfloat16)

    def out_copies():
        for k in range(16):
            target = (hb, k, 4 * j + x)
            yield is_me(*target), target, O.at[k], ors.at[k]

    dst, arrive = R.at[bl_me, 2 * y + h], orr.at[bl_me, 2 * y + h]
    for me, target, src, sem in out_copies():
        @pl.when(jnp.logical_not(me))
        def _(src=src, sem=sem, target=target):
            send(src, dst, sem, arrive, target).start()
        @pl.when(me)
        def _(src=src):
            pltpu.make_async_copy(src, dst, arrive).start()

    for bl in range(2):
        for g in range(8):
            send(O.at[0], R.at[bl, g], ors.at[0], orr.at[bl, g], sib).wait_recv()
        for n, out in enumerate((out_s, out_r)):
            for part in range(2):
                tile = jnp.concatenate(
                    [R[bl, g, n, 16 * part:16 * part + 16, :].astype(jnp.float32) for g in range(8)], axis=0)
                out[bl, part] = tile.T

    @pl.when(chosen)
    def _():
        for me, target, src, sem in tile_copies():
            @pl.when(jnp.logical_not(me))
            def _(src=src, sem=sem, target=target):
                send(src, W.at[i, t], sem, zr.at[t], target).wait_send()
    for me, target, src, sem, to in rhs_copies():
        @pl.when(jnp.logical_not(me))
        def _(src=src, sem=sem, to=to, target=target):
            send(src, to, sem, br.at[i], target).wait_send()
    for me, target, src, sem in out_copies():
        @pl.when(jnp.logical_not(me))
        def _(src=src, sem=sem, target=target):
            send(src, dst, sem, arrive, target).wait_send()
    for d in range(5):
        first, second = axes(d)
        def own(d=d):
            for n in range(11):
                panel_send(i, d, n, step_x(i, 1)).wait_send()
        when(row_ok(d, i), own)
        for e in range(4):
            def passed(d=d, e=e):
                panel_send(i, d, 11 + e, step_x(i, 1)).wait_send()
            when(row_ok(d, second(i, forward_side(d, e))), passed)
    for it in range(ITERS):
        send(X.at[it, h], X.at[it, h], xs.at[it], xr.at[it], sib).wait_send()


def local(gamma, rhs):
    vmem = pl.BlockSpec(memory_space=pltpu.VMEM)
    dma = pltpu.SemaphoreType.DMA
    f32, bf16 = jnp.float32, jnp.bfloat16
    shape = jax.ShapeDtypeStruct(rhs.shape, f32)
    return pl.pallas_call(
        kernel,
        out_shape=(shape, shape),
        in_specs=[vmem, vmem],
        out_specs=(vmem, vmem),
        scratch_shapes=[
            pltpu.VMEM((16, 10, T, T), bf16),
            pltpu.VMEM((2, 8, 32, T), f32),
            pltpu.VMEM((16, 32, T), f32),
            pltpu.VMEM((ITERS, 2, 16, 32, T), bf16),
            pltpu.VMEM((16, 64, T), bf16),
            pltpu.VMEM((2, 32, N), f32),
            pltpu.VMEM((ITERS, 32, N), f32),
            pltpu.VMEM((2, 8, T), f32),
            pltpu.VMEM((32, N), f32),
            pltpu.VMEM((32, N), f32),
            pltpu.VMEM((32, N), f32),
            pltpu.VMEM((32, N), f32),
            pltpu.VMEM((16, 2, 32, T), bf16),
            pltpu.VMEM((2, 8, 2, 32, T), bf16),
            dma((10,)), dma((16,)), dma((16,)), dma((16,)), dma((16, 5)), dma((5, 15)),
            dma((ITERS,)), dma((ITERS,)), dma((ITERS,)), dma((ITERS,)), dma((1,)), dma((1,)),
            dma((2, 8)), dma((16,)),
        ],
        compiler_params=pltpu.CompilerParams(
            collective_id=0, has_side_effects=True, vmem_limit_bytes=40 * 2**20),
    )(gamma, rhs)


def solution(mesh):
    spec = P("bin", None, "row", "col")
    return jax.shard_map(local, mesh=mesh, in_specs=(spec, spec), out_specs=(spec, spec), check_vma=False)
```

```python
import jax
import jax.numpy as jnp
from jax import lax
from jax.experimental import pallas as pl
from jax.experimental.pallas import tpu as pltpu
from jax.sharding import PartitionSpec as P

MESH = pl.DeviceIdType.MESH
N = 2048
ITERS = 3
EPS_REL = 0.1
T = 128
SB = 8
APART = (0, 3, 6, 1, 4)
CHUNKS = ((0, 2), (2, 4), (4, 6), (6, 8), (8, 9), (9, 10))


def kernel(gamma, rhs, out_s, out_r,
           W, tile_in, bT, B, X, Xs, Y, Z, shs, dir_, res, sol, img, O, R,
           zr, zs, ws, br, bs, rs, ss, xr, xs, yr, ys, shr_sem, shs_sem, orr, ors, in_sem):
    h = lax.axis_index("bin")
    i = lax.axis_index("row")
    z = lax.axis_index("col")
    y, x = i // 4, i % 4
    hb, bl_me = (z % 4) // 2, z % 2
    big = i // 2
    home = (z + 17 - x) % 16

    fetch = pltpu.make_async_copy(rhs, tile_in, in_sem.at[0])
    fetch.start()

    def dev(b, r, c):
        return {"bin": b, "row": r, "col": c}

    def is_me(b, r, c):
        return (b == h) & (r == i) & (c == z)

    def step_x(row, d):
        return (row // 4) * 4 + (row % 4 + d) % 4

    def step_y(row, d):
        return (row // 4 + d) % 4 * 4 + row % 4

    def step_z(d):
        return (z + d + 16) % 16

    barrier = pltpu.get_barrier_semaphore()

    def greet(b, r, c, maybe_me):
        def far():
            pl.semaphore_signal(barrier, inc=1, device_id=dev(b, r, c), device_id_type=MESH)
        if maybe_me:
            pl.when(jnp.logical_not(is_me(b, r, c)))(far)
        else:
            far()

    for d in (4, -4):
        greet(hb, i, step_z(d), False)
        greet(h, i, step_z(d), False)
    for d in (3, -3, 2, -2, 1, -1):
        greet(hb, i, step_z(d), False)
    greet(hb, i, z, True)
    for k in range(16):
        greet(hb, k, home, True)
    for d in (1, 2, 3):
        greet(h, step_x(i, d), z, False)
        greet(h, step_y(i, d), z, False)
    greet(1 - h, i, z, False)

    fetch.wait()
    for bl in range(2):
        for part in range(2):
            tile = tile_in[bl, part].T
            for g in range(8):
                bT[bl, g, 16 * part:16 * part + 16, :] = tile[16 * g:16 * g + 16, :]

    mine = jnp.where(h == hb, 1, 0)
    pl.semaphore_wait(barrier, 33 + mine - mine * jnp.where(x == 1, 1, 0))

    def send(src, dst, send_sem, recv_sem, target):
        return pltpu.make_async_remote_copy(
            src_ref=src, dst_ref=dst, send_sem=send_sem, recv_sem=recv_sem,
            device_id=dev(*target), device_id_type=MESH)

    sib = (1 - h, i, z)

    apart = (z // 2 - big + 8) % 8
    slot = jnp.where(apart == 0, 0, jnp.where(apart == 3, 1, jnp.where(apart == 6, 2, jnp.where(apart == 1, 3, 4))))
    chosen = (slot < 4) | ((apart == 4) & (big < 4))
    t = 2 * slot + z % 2

    def tile_copies():
        n = 0
        for bl in range(2):
            ahead = (2 * h + bl + 4 - z % 4) % 4
            for q in range(2):
                for kind in range(3):
                    if kind == 0:
                        target, cond = (q, i, step_z(ahead)), jnp.logical_not((ahead == 0) & (q == h))
                    elif kind == 1:
                        target, cond = (q, i, step_z(ahead - 4)), True
                    else:
                        target, cond = (q, i, step_z(4)), ahead == 0
                    yield cond, target, gamma.at[bl, q], zs.at[n]
                    n += 1

    def when(cond, body):
        if cond is True:
            body()
        else:
            pl.when(cond)(body)

    def send_tiles():
        for cond, target, src, sem in tile_copies():
            when(cond, lambda: send(src, W.at[i, t], sem, zr.at[t], target).start())
        @pl.when(h == hb)
        def _():
            pltpu.make_async_copy(gamma.at[bl_me, h], W.at[i, t], zr.at[t]).start()

    def tile_wait(u):
        send(gamma.at[0, 0], W.at[i, u], zs.at[0], zr.at[u], sib).wait_recv()

    def route(u):
        off = (z - 2 * (big + APART[u // 2]) - u % 2 + 32) % 16
        up = ((off >= 1) & (off <= 3)) | ((off == 4) & (h == 0))
        down = (off >= 13) | ((off == 12) & (h == 1))
        near = (off <= 4) | (off >= 12)
        return near, up | down, (h, i, step_z(jnp.where(up, 4, -4)))

    def tile_pass(u, target):
        return send(W.at[i, u], W.at[i, u], ws.at[u], zr.at[u], target)

    def slot_ok(u, row):
        return True if u < 8 else row < 8

    def both_conds(a, b):
        return a if b is True else a & b

    def near_tiles(slots):
        for u in slots:
            near, relay, target = route(u)
            @pl.when(both_conds(near, slot_ok(u, i)))
            def _(u=u, relay=relay, target=target):
                tile_wait(u)
                @pl.when(relay)
                def _():
                    tile_pass(u, target).start()

    def far_tiles(slots):
        for u in slots:
            near, _, _ = route(u)
            @pl.when(both_conds(jnp.logical_not(near), slot_ok(u, i)))
            def _(u=u):
                tile_wait(u)

    def rhs_copies():
        n = 0
        for bl in range(2):
            xx = (2 * h + bl + 5 - z % 4) % 4
            for yy in range(4):
                for q in range(2):
                    target = (q, 4 * yy + xx, (z + 15 + xx) % 16)
                    yield is_me(*target), target, bT.at[bl, 2 * yy + q], bs.at[n]
                    n += 1

    def send_rhs():
        for me, target, src, sem in rhs_copies():
            pl.when(jnp.logical_not(me))(lambda: send(src, B.at[i], sem, br.at[i], target).start())
            pl.when(me)(lambda: pltpu.make_async_copy(src, B.at[i], br.at[i]).start())

    def panel(row, c):
        a, b = CHUNKS[c]
        return W.at[row, a:b]

    def panel_send(row, c, n, target_row):
        return send(panel(row, c), panel(row, c), ss.at[c, n], rs.at[row, c], (h, target_row, z))

    def panel_wait(row, c):
        panel_send(row, c, 0, step_x(i, 1)).wait_recv()

    def axes(c):
        return (step_x, step_y) if c % 2 == 0 else (step_y, step_x)

    def row_ok(c, row):
        return True if c < 4 else row < 8

    def forward_side(c, e):
        return 1 if (c // 2 + e) % 2 == 0 else 3

    def stage_a(c):
        first, second = axes(c)
        def body():
            for n, e in enumerate((1, 3, 2)):
                panel_send(i, c, n, first(i, e)).start()
            for n, e in enumerate((1, 3)):
                panel_send(i, c, 3 + n, second(i, e)).start()
        when(row_ok(c, i), body)

    def stage_b(c):
        first, second = axes(c)
        for n, e in enumerate((1, 3, 2)):
            row = first(i, e)
            def body(n=n, row=row):
                panel_wait(row, c)
                for m, f in enumerate((1, 3)):
                    panel_send(row, c, 5 + 2 * n + m, second(i, f)).start()
            when(row_ok(c, row), body)

    def stage_c(c):
        first, second = axes(c)
        for side in (1, 3):
            for e in range(4):
                row = first(second(i, side), e)
                def body(side=side, e=e, row=row):
                    panel_wait(row, c)
                    if forward_side(c, e) == side:
                        panel_send(row, c, 11 + e, second(i, 4 - side)).start()
                when(row_ok(c, row), body)

    def stage_e(c):
        first, second = axes(c)
        for e in range(4):
            row = first(second(i, 2), e)
            when(row_ok(c, row), lambda: panel_wait(row, c))

    def x_copy(it):
        return send(X.at[it, h], X.at[it, h], xs.at[it], xr.at[it], sib)

    sign = jnp.where(h == 0, 1.0, -1.0).astype(jnp.bfloat16)

    def x_ready(it):
        x_copy(it).wait_recv()
        for k in range(16):
            Xs[k] = X[it, :, k].reshape(64, T) * sign

    def rhs_arrived():
        for k in range(16):
            send(bT.at[0, 0], B.at[k], bs.at[0], br.at[k], sib).wait_recv()
            X[0, h, k] = B[k].astype(jnp.bfloat16)
        x_copy(0).start()
        for k in range(16):
            cols = slice(T * k, T * k + T)
            dir_[:, cols] = B[k]
            res[:, cols] = B[k]
        sol[...] = jnp.zeros_like(sol)

    def super_tile(a, n):
        return jnp.concatenate(
            [jnp.concatenate([W[2 * a, 2 * n], W[2 * a, 2 * n + 1]], axis=1),
             jnp.concatenate([W[2 * a + 1, 2 * n], W[2 * a + 1, 2 * n + 1]], axis=1)], axis=0)

    def products(it, c, n, acc):
        def add(acc, v):
            return v if acc is None else acc + v
        d = APART[n]
        a = (c - d) % SB
        if n < 4 or a < 4:
            left = jnp.concatenate([Xs[2 * a], Xs[2 * a + 1]], axis=1)
            acc = add(acc, jnp.dot(left, super_tile(a, n), preferred_element_type=jnp.float32))
        k = (c + d) % SB
        if n > 0 and (n < 4 or c < 4):
            left = jnp.concatenate([X[it, :, 2 * k].reshape(64, T), X[it, :, 2 * k + 1].reshape(64, T)], axis=1)
            acc = add(acc, lax.dot_general(
                left, super_tile(c, n), (((1,), (1,)), ((), ())), preferred_element_type=jnp.float32))
        return acc

    def y_copy(it, c):
        return send(Y.at[1 - h, c], Z.at[it, c], ys.at[it, c], yr.at[it, c], sib)

    def first_product(n):
        for c in range(SB):
            acc = products(0, c, n, None if n == 0 else Y[:, c].reshape(64, 256))
            Y[:, c] = acc.reshape(2, 32, 256)
            if n == 4:
                y_copy(0, c).start()

    first_slots, later_slots = range(4), range(4, 10)

    pl.when(chosen & (slot < 2))(send_tiles)
    send_rhs()
    near_tiles(first_slots)
    far_tiles((0, 1))
    stage_a(0)
    far_tiles((2, 3))
    stage_a(1)
    pl.when(chosen & (slot >= 2))(send_tiles)
    stage_b(0)
    stage_b(1)
    rhs_arrived()
    near_tiles(later_slots)
    stage_c(0)
    far_tiles((4, 5))
    stage_a(2)
    far_tiles((6, 7))
    stage_a(3)
    far_tiles((8, 9))
    stage_a(4)
    stage_a(5)
    stage_c(1)
    for c in range(2, 6):
        stage_b(c)
    stage_e(0)
    x_ready(0)
    first_product(0)
    stage_e(1)
    stage_c(2)
    stage_c(3)
    first_product(1)

    total = jnp.zeros((T, T), jnp.float32)
    for k in range(16):
        total = total + W[k, k % 2].astype(jnp.float32)
    eye = lax.broadcasted_iota(jnp.int32, (T, T), 0) == lax.broadcasted_iota(jnp.int32, (T, T), 1)
    total = jnp.where(eye, total, 0.0)
    trace = jnp.sum(jnp.sum(total, axis=0, keepdims=True), axis=1, keepdims=True)
    shs[0] = jnp.broadcast_to(EPS_REL * trace / N, (8, T))
    shift_copy = send(shs.at[0], shs.at[1], shs_sem.at[0], shr_sem.at[0], sib)
    shift_copy.start()

    stage_c(4)
    stage_c(5)
    stage_e(2)
    first_product(2)
    stage_e(3)
    first_product(3)
    stage_e(4)
    stage_e(5)
    first_product(4)

    def both(v):
        s = v[:16] + v[16:]
        return jnp.concatenate([s, s], axis=0)

    def row_sum(parts):
        total = parts[0]
        for p in parts[1:]:
            total = total + p
        return both(jnp.sum(total, axis=1, keepdims=True))

    slabs = [slice(256 * c, 256 * c + 256) for c in range(SB)]
    rr0 = row_sum([res[:, s] * res[:, s] for s in slabs])
    shift_copy.wait()
    shift = jnp.where(h == 0, shs[0], shs[1])[:1, :1]

    def iteration(it, rr):
        curve = []
        for c, s in enumerate(slabs):
            y_copy(it, c).wait()
            own, other = Y[h, c], Z[it, c]
            real = jnp.where(h == 0, own, other)
            imag = jnp.where(h == 0, other, own)
            d = dir_[:, s]
            image = real + jnp.concatenate([-imag[16:], imag[:16]], axis=0) + shift * d
            img[:, s] = image
            curve.append(d * image)
        alpha = rr / row_sum(curve)
        norm = []
        for s in slabs:
            sol[:, s] = sol[:, s] + alpha * dir_[:, s]
            r = res[:, s] - alpha * img[:, s]
            res[:, s] = r
            norm.append(r * r)
        new = row_sum(norm)

        @pl.when(it + 1 < ITERS)
        def _():
            beta = new / rr
            for k in range(16):
                cols = slice(T * k, T * k + T)
                d = res[:, cols] + beta * dir_[:, cols]
                dir_[:, cols] = d
                X[it + 1, h, k] = d.astype(jnp.bfloat16)
            x_copy(it + 1).start()
            x_ready(it + 1)
            for c in range(SB):
                acc = None
                for n in range(5):
                    acc = products(it + 1, c, n, acc)
                Y[:, c] = acc.reshape(2, 32, 256)
                y_copy(it + 1, c).start()

        return new

    lax.fori_loop(0, ITERS, iteration, rr0)

    dst, arrive = R.at[bl_me, 2 * y + h], orr.at[bl_me, 2 * y + h]

    def out_copies():
        for k in range(16):
            target = (hb, k, home)
            yield is_me(*target), target, O.at[k], ors.at[k], k

    for me, target, src, sem, k in out_copies():
        cols = slice(T * k, T * k + T)
        O[k, 0] = sol[:, cols].astype(jnp.bfloat16)
        O[k, 1] = res[:, cols].astype(jnp.bfloat16)
        pl.when(jnp.logical_not(me))(lambda: send(src, dst, sem, arrive, target).start())
        pl.when(me)(lambda: pltpu.make_async_copy(src, dst, arrive).start())

    for bl in range(2):
        for g in range(8):
            send(O.at[0], R.at[bl, g], ors.at[0], orr.at[bl, g], sib).wait_recv()
        for n, out in enumerate((out_s, out_r)):
            for part in range(2):
                tile = jnp.concatenate(
                    [R[bl, g, n, 16 * part:16 * part + 16, :].astype(jnp.float32) for g in range(8)], axis=0)
                out[bl, part] = tile.T

    @pl.when(chosen)
    def _():
        for cond, target, src, sem in tile_copies():
            when(cond, lambda: send(src, W.at[i, t], sem, zr.at[t], target).wait_send())
    for u in range(10):
        _, relay, target = route(u)
        pl.when(both_conds(relay, slot_ok(u, i)))(lambda: tile_pass(u, target).wait_send())
    for me, target, src, sem in rhs_copies():
        pl.when(jnp.logical_not(me))(lambda: send(src, B.at[i], sem, br.at[i], target).wait_send())
    for me, target, src, sem, k in out_copies():
        pl.when(jnp.logical_not(me))(lambda: send(src, dst, sem, arrive, target).wait_send())
    for c in range(6):
        first, second = axes(c)
        def own():
            for n in range(5):
                panel_send(i, c, n, step_x(i, 1)).wait_send()
        when(row_ok(c, i), own)
        for n, e in enumerate((1, 3, 2)):
            def peer():
                for m in range(2):
                    panel_send(i, c, 5 + 2 * n + m, step_x(i, 1)).wait_send()
            when(row_ok(c, first(i, e)), peer)
        for e in range(4):
            row = first(second(i, forward_side(c, e)), e)
            when(row_ok(c, row), lambda: panel_send(i, c, 11 + e, step_x(i, 1)).wait_send())
    for it in range(ITERS):
        x_copy(it).wait_send()


def local(gamma, rhs):
    vmem = pl.BlockSpec(memory_space=pltpu.VMEM)
    dma = pltpu.SemaphoreType.DMA
    f32, bf16 = jnp.float32, jnp.bfloat16
    shape = jax.ShapeDtypeStruct(rhs.shape, f32)
    return pl.pallas_call(
        kernel,
        out_shape=(shape, shape),
        in_specs=[pl.BlockSpec(memory_space=pl.ANY)] * 2,
        out_specs=(vmem, vmem),
        scratch_shapes=[
            pltpu.VMEM((16, 10, T, T), bf16),
            pltpu.VMEM((2, 2, T, T), f32),
            pltpu.VMEM((2, 8, 32, T), f32),
            pltpu.VMEM((16, 32, T), f32),
            pltpu.VMEM((ITERS, 2, 16, 32, T), bf16),
            pltpu.VMEM((16, 64, T), bf16),
            pltpu.VMEM((2, SB, 32, 256), f32),
            pltpu.VMEM((ITERS, SB, 32, 256), f32),
            pltpu.VMEM((2, 8, T), f32),
            pltpu.VMEM((32, N), f32),
            pltpu.VMEM((32, N), f32),
            pltpu.VMEM((32, N), f32),
            pltpu.VMEM((32, N), f32),
            pltpu.VMEM((16, 2, 32, T), bf16),
            pltpu.VMEM((2, 8, 2, 32, T), bf16),
            dma((10,)), dma((12,)), dma((10,)), dma((16,)), dma((16,)), dma((16, 6)), dma((6, 15)),
            dma((ITERS,)), dma((ITERS,)), dma((ITERS, SB)), dma((ITERS, SB)), dma((1,)), dma((1,)),
            dma((2, 8)), dma((16,)), dma((1,)),
        ],
        compiler_params=pltpu.CompilerParams(
            collective_id=0, has_side_effects=True, vmem_limit_bytes=60 * 2**20),
    )(gamma, rhs)


def solution(mesh):
    spec = P("bin", None, "row", "col")
    return jax.shard_map(local, mesh=mesh, in_specs=(spec, spec), out_specs=(spec, spec), check_vma=False)
```

```python
import jax
import jax.numpy as jnp
from jax import lax
from jax.experimental import pallas as pl
from jax.experimental.pallas import tpu as pltpu
from jax.sharding import PartitionSpec as P

MESH = pl.DeviceIdType.MESH
N = 2048
ITERS = 3
EPS_REL = 0.1
T = 128
SB = 8
FAR_FIRST = ((2, 2), (2, 1), (2, 3), (1, 2), (3, 2), (1, 1), (1, 3), (3, 1), (3, 3), (2, 0), (0, 2), (1, 0), (3, 0), (0, 1), (0, 3), (0, 0))
APART = (0, 3, 6, 1, 4)
CHUNKS = ((0, 2), (2, 4), (4, 6), (6, 8), (8, 9), (9, 10))


def kernel(gamma, rhs, out,
           W, tile_in, bT, B, X, Xs, Y, Z, shs, dir_, res, sol, img, O, R,
           zr, zs, ws, br, bs, rs, gs, ss, xr, xs, yr, ys, shr_sem, shs_sem, orr, ors, in_sem):
    h = lax.axis_index("bin")
    i = lax.axis_index("row")
    z = lax.axis_index("col")
    y, x = i // 4, i % 4
    hb, bl_me = (z % 4) // 2, z % 2
    big = i // 2
    home = (z + 17 - x) % 16

    fetch = pltpu.make_async_copy(rhs, tile_in, in_sem.at[0])
    fetch.start()

    def dev(b, r, c):
        return {"bin": b, "row": r, "col": c}

    def is_me(b, r, c):
        return (b == h) & (r == i) & (c == z)

    def step_x(row, d):
        return (row // 4) * 4 + (row % 4 + d) % 4

    def step_y(row, d):
        return (row // 4 + d) % 4 * 4 + row % 4

    def step_z(d):
        return (z + d + 16) % 16

    barrier = pltpu.get_barrier_semaphore()

    def greet(b, r, c, maybe_me):
        def far():
            pl.semaphore_signal(barrier, inc=1, device_id=dev(b, r, c), device_id_type=MESH)
        if maybe_me:
            pl.when(jnp.logical_not(is_me(b, r, c)))(far)
        else:
            far()

    for d in (4, -4):
        greet(hb, i, step_z(d), False)
        greet(h, i, step_z(d), False)
    for d in (3, -3, 2, -2, 1, -1):
        greet(hb, i, step_z(d), False)
    greet(hb, i, z, True)
    for k in range(16):
        greet(hb, k, home, True)
    for d in (1, 2, 3):
        greet(h, step_x(i, d), z, False)
        greet(h, step_y(i, d), z, False)
    greet(1 - h, i, z, False)

    mine = jnp.where(h == hb, 1, 0)
    pl.semaphore_wait(barrier, 33 + mine - mine * jnp.where(x == 1, 1, 0))

    def send(src, dst, send_sem, recv_sem, target):
        return pltpu.make_async_remote_copy(
            src_ref=src, dst_ref=dst, send_sem=send_sem, recv_sem=recv_sem,
            device_id=dev(*target), device_id_type=MESH)

    sib = (1 - h, i, z)

    apart = (z // 2 - big + 8) % 8
    slot = jnp.where(apart == 0, 0, jnp.where(apart == 3, 1, jnp.where(apart == 6, 2, jnp.where(apart == 1, 3, 4))))
    chosen = (slot < 4) | ((apart == 4) & (big < 4))
    t = 2 * slot + z % 2

    def tile_copies():
        n = 0
        for bl in range(2):
            ahead = (2 * h + bl + 4 - z % 4) % 4
            for q in range(2):
                for kind in range(3):
                    if kind == 0:
                        target, cond = (q, i, step_z(ahead)), jnp.logical_not((ahead == 0) & (q == h))
                    elif kind == 1:
                        target, cond = (q, i, step_z(ahead - 4)), True
                    else:
                        target, cond = (q, i, step_z(4)), ahead == 0
                    yield cond, target, gamma.at[bl, q], zs.at[n]
                    n += 1

    def when(cond, body):
        if cond is True:
            body()
        else:
            pl.when(cond)(body)

    def send_tiles():
        for cond, target, src, sem in tile_copies():
            when(cond, lambda: send(src, W.at[y, x, t], sem, zr.at[t], target).start())
        @pl.when(h == hb)
        def _():
            pltpu.make_async_copy(gamma.at[bl_me, h], W.at[y, x, t], zr.at[t]).start()

    def tile_wait(u):
        send(gamma.at[0, 0], W.at[y, x, u], zs.at[0], zr.at[u], sib).wait_recv()

    def route(u):
        off = (z - 2 * (big + APART[u // 2]) - u % 2 + 32) % 16
        up = ((off >= 1) & (off <= 3)) | ((off == 4) & (h == 0))
        down = (off >= 13) | ((off == 12) & (h == 1))
        near = (off <= 4) | (off >= 12)
        return near, up | down, (h, i, step_z(jnp.where(up, 4, -4)))

    def tile_pass(u, target):
        return send(W.at[y, x, u], W.at[y, x, u], ws.at[u], zr.at[u], target)

    def slot_ok(u, row):
        return True if u < 8 else row < 8

    def both_conds(a, b):
        return a if b is True else a & b

    def near_tiles(slots):
        for u in slots:
            near, relay, target = route(u)
            @pl.when(both_conds(near, slot_ok(u, i)))
            def _(u=u, relay=relay, target=target):
                tile_wait(u)
                @pl.when(relay)
                def _():
                    tile_pass(u, target).start()

    def far_tiles(slots):
        for u in slots:
            near, _, _ = route(u)
            @pl.when(both_conds(jnp.logical_not(near), slot_ok(u, i)))
            def _(u=u):
                tile_wait(u)

    def turn_rhs():
        fetch.wait()
        for bl in range(2):
            for part in range(2):
                tile = tile_in[bl, part].T
                for g in range(8):
                    bT[bl, g, 16 * part:16 * part + 16, :] = tile[16 * g:16 * g + 16, :]

    def rhs_copies():
        n = 0
        for bl in range(2):
            xx = (2 * h + bl + 5 - z % 4) % 4
            for yy in range(4):
                for q in range(2):
                    target = (q, 4 * yy + xx, (z + 15 + xx) % 16)
                    yield is_me(*target), target, bT.at[bl, 2 * yy + q], bs.at[n]
                    n += 1

    def send_rhs():
        for me, target, src, sem in rhs_copies():
            pl.when(jnp.logical_not(me))(lambda: send(src, B.at[i], sem, br.at[i], target).start())
            pl.when(me)(lambda: pltpu.make_async_copy(src, B.at[i], br.at[i]).start())

    def panel_send(row, c, n, target_row, part=None):
        a, b = CHUNKS[c]
        rows = slice(0, T) if part is None else slice(part * T // 2, (part + 1) * T // 2)
        ref = W.at[row // 4, row % 4, a:b, rows]
        arrive = rs.at[row, c, 0 if part is None else part]
        return send(ref, ref, ss.at[c, n], arrive, (h, target_row, z))

    def group_send(line, c, n, part, sem, target_row):
        a, b = CHUNKS[c]
        size = 2 if c == 5 else 4
        lo, hi = (0, size) if part is None else (part * size // 2, (part + 1) * size // 2)
        ref = W.at[line, lo:hi, a:b] if c % 2 == 0 else W.at[lo:hi, line, a:b]
        return send(ref, ref, ss.at[c, n], gs.at[c, sem], (h, target_row, z))

    def axes(c):
        return (step_x, step_y) if c % 2 == 0 else (step_y, step_x)

    def line_of(c, row):
        return row // 4 if c % 2 == 0 else row % 4

    def row_ok(c, row):
        return True if c < 4 else row < 8

    def line_ok(c, line):
        return line < 2 if c == 4 else True

    def stage_a(c):
        first, _ = axes(c)
        def body():
            for n, e in enumerate((1, 3)):
                panel_send(i, c, n, first(i, e)).start()
        when(row_ok(c, i), body)

    def stage_f(c):
        first, _ = axes(c)
        for e, part in ((1, 0), (3, 1)):
            row = first(i, e)
            def body():
                panel_send(row, c, 0, first(i, 1)).wait_recv()
                panel_send(row, c, 2 + 5 * part, first(i, 4 - e), part).start()
            when(row_ok(c, row), body)

    def stage_b(c):
        first, second = axes(c)
        row = first(i, 2)
        def halves():
            for part in range(2):
                panel_send(row, c, 0, first(i, 1), part).wait_recv()
        when(row_ok(c, row), halves)
        line = line_of(c, i)
        def body():
            group_send(line, c, 3, None, 1, second(i, 1)).start()
            group_send(line, c, 4, None, 0, second(i, 3)).start()
        when(line_ok(c, line), body)

    def stage_c(c):
        _, second = axes(c)
        for side, part in ((1, 0), (3, 1)):
            line = line_of(c, second(i, side))
            def body():
                group_send(line, c, 3, None, part, second(i, 1)).wait_recv()
                group_send(line, c, 5 + part, part, 2 + part, second(i, 4 - side)).start()
            when(line_ok(c, line), body)

    def stage_e(c):
        _, second = axes(c)
        line = line_of(c, second(i, 2))
        def body():
            for part in range(2):
                group_send(line, c, 3, part, 2 + part, second(i, 1)).wait_recv()
        when(line_ok(c, line), body)

    def x_copy(it):
        return send(X.at[it, h], X.at[it, h], xs.at[it], xr.at[it], sib)

    sign = jnp.where(h == 0, 1.0, -1.0).astype(jnp.bfloat16)

    def x_ready(it):
        x_copy(it).wait_recv()
        for k in range(16):
            Xs[k] = X[it, :, k].reshape(64, T) * sign

    def rhs_arrived():
        for k in range(16):
            send(bT.at[0, 0], B.at[k], bs.at[0], br.at[k], sib).wait_recv()
            X[0, h, k] = B[k].astype(jnp.bfloat16)
        x_copy(0).start()
        for k in range(16):
            cols = slice(T * k, T * k + T)
            dir_[:, cols] = B[k]
            res[:, cols] = B[k]
        sol[...] = jnp.zeros_like(sol)

    def super_tile(a, n):
        return jnp.concatenate(
            [jnp.concatenate([W[a // 2, r, 2 * n], W[a // 2, r, 2 * n + 1]], axis=1)
             for r in (2 * (a % 2), 2 * (a % 2) + 1)], axis=0)

    def products(it, c, n, acc):
        def add(acc, v):
            return v if acc is None else acc + v
        d = APART[n]
        a = (c - d) % SB
        if n < 4 or a < 4:
            left = jnp.concatenate([Xs[2 * a], Xs[2 * a + 1]], axis=1)
            acc = add(acc, jnp.dot(left, super_tile(a, n), preferred_element_type=jnp.float32))
        k = (c + d) % SB
        if n > 0 and (n < 4 or c < 4):
            left = jnp.concatenate([X[it, :, 2 * k].reshape(64, T), X[it, :, 2 * k + 1].reshape(64, T)], axis=1)
            acc = add(acc, lax.dot_general(
                left, super_tile(c, n), (((1,), (1,)), ((), ())), preferred_element_type=jnp.float32))
        return acc

    def y_copy(it):
        return send(Y.at[1 - h], Z.at[it], ys.at[it], yr.at[it], sib)

    def first_product(n):
        for c in range(SB):
            acc = products(0, c, n, None if n == 0 else Y[:, c].reshape(64, 256))
            Y[:, c] = acc.reshape(2, 32, 256)

    pl.when(chosen)(send_tiles)
    turn_rhs()
    send_rhs()
    near_tiles(range(10))
    for c in range(6):
        far_tiles(range(*CHUNKS[c]))
        stage_a(c)
    for c in range(6):
        stage_f(c)
    rhs_arrived()
    for c in range(6):
        stage_b(c)
    for c in range(6):
        stage_c(c)
    x_ready(0)
    for c in range(4):
        stage_e(c)
        first_product(c)
    stage_e(4)
    stage_e(5)
    first_product(4)
    y_copy(0).start()

    total = jnp.zeros((T, T), jnp.float32)
    for k in range(16):
        total = total + W[k // 4, k % 4, k % 2].astype(jnp.float32)
    eye = lax.broadcasted_iota(jnp.int32, (T, T), 0) == lax.broadcasted_iota(jnp.int32, (T, T), 1)
    total = jnp.where(eye, total, 0.0)
    trace = jnp.sum(jnp.sum(total, axis=0, keepdims=True), axis=1, keepdims=True)
    shs[0] = jnp.broadcast_to(EPS_REL * trace / N, (8, T))
    shift_copy = send(shs.at[0], shs.at[1], shs_sem.at[0], shr_sem.at[0], sib)
    shift_copy.start()

    def both(v):
        s = v[:16] + v[16:]
        return jnp.concatenate([s, s], axis=0)

    def row_sum(parts):
        total = parts[0]
        for p in parts[1:]:
            total = total + p
        return both(jnp.sum(total, axis=1, keepdims=True))

    slabs = [slice(256 * c, 256 * c + 256) for c in range(SB)]
    rr0 = row_sum([res[:, s] * res[:, s] for s in slabs])
    shift_copy.wait()
    shift = jnp.where(h == 0, shs[0], shs[1])[:1, :1]

    def iteration(it, rr):
        y_copy(it).wait()
        curve = []
        for c, s in enumerate(slabs):
            own, other = Y[h, c], Z[it, c]
            real = jnp.where(h == 0, own, other)
            imag = jnp.where(h == 0, other, own)
            d = dir_[:, s]
            image = real + jnp.concatenate([-imag[16:], imag[:16]], axis=0) + shift * d
            img[:, s] = image
            curve.append(d * image)
        alpha = rr / row_sum(curve)
        norm = []
        for s in slabs:
            sol[:, s] = sol[:, s] + alpha * dir_[:, s]
            r = res[:, s] - alpha * img[:, s]
            res[:, s] = r
            norm.append(r * r)
        new = row_sum(norm)

        @pl.when(it + 1 < ITERS)
        def _():
            beta = new / rr
            for k in range(16):
                cols = slice(T * k, T * k + T)
                d = res[:, cols] + beta * dir_[:, cols]
                dir_[:, cols] = d
                X[it + 1, h, k] = d.astype(jnp.bfloat16)
            x_copy(it + 1).start()
            x_ready(it + 1)
            for c in range(SB):
                acc = None
                for n in range(5):
                    acc = products(it + 1, c, n, acc)
                Y[:, c] = acc.reshape(2, 32, 256)
            y_copy(it + 1).start()

        return new

    lax.fori_loop(0, ITERS, iteration, rr0)

    dst, arrive = R.at[bl_me, 2 * y + h], orr.at[bl_me, 2 * y + h]

    def out_copies():
        for n, (dy, dx) in enumerate(FAR_FIRST):
            row = step_y(step_x(i, dx), dy)
            target = (hb, row, home)
            yield (is_me(*target) if dx + dy == 0 else None), target, O.at[row], ors.at[n]

    for k in range(16):
        cols = slice(T * k, T * k + T)
        O[k, 0] = sol[:, cols].astype(jnp.bfloat16)
        O[k, 1] = res[:, cols].astype(jnp.bfloat16)
    for me, target, src, sem in out_copies():
        go = lambda: send(src, dst, sem, arrive, target).start()
        if me is None:
            go()
        else:
            pl.when(jnp.logical_not(me))(go)
            pl.when(me)(lambda: pltpu.make_async_copy(src, dst, arrive).start())

    for bl in range(2):
        for g in range(8):
            send(O.at[0], R.at[bl, g], ors.at[0], orr.at[bl, g], sib).wait_recv()
    out[...] = R[...]

    @pl.when(chosen)
    def _():
        for cond, target, src, sem in tile_copies():
            when(cond, lambda: send(src, W.at[y, x, t], sem, zr.at[t], target).wait_send())
    for u in range(10):
        _, relay, target = route(u)
        pl.when(both_conds(relay, slot_ok(u, i)))(lambda: tile_pass(u, target).wait_send())
    for me, target, src, sem in rhs_copies():
        pl.when(jnp.logical_not(me))(lambda: send(src, B.at[i], sem, br.at[i], target).wait_send())
    for me, target, src, sem in out_copies():
        when(True if me is None else jnp.logical_not(me), lambda: send(src, dst, sem, arrive, target).wait_send())
    for c in range(6):
        first, second = axes(c)
        def own():
            for n in range(2):
                panel_send(i, c, n, step_x(i, 1)).wait_send()
        when(row_ok(c, i), own)
        for e, part in ((1, 0), (3, 1)):
            row = first(i, e)
            when(row_ok(c, row), lambda: panel_send(row, c, 2 + 5 * part, step_x(i, 1), part).wait_send())
        line = line_of(c, i)
        def group():
            for n in (3, 4):
                group_send(line, c, n, None, 0, step_x(i, 1)).wait_send()
        when(line_ok(c, line), group)
        for side, part in ((1, 0), (3, 1)):
            line = line_of(c, second(i, side))
            when(line_ok(c, line), lambda: group_send(line, c, 5 + part, part, 0, step_x(i, 1)).wait_send())
    for it in range(ITERS):
        x_copy(it).wait_send()


def turn_back(r, out_s, out_r):
    for bl in range(2):
        for n, out in enumerate((out_s, out_r)):
            for part in range(2):
                tile = jnp.concatenate(
                    [r[bl, g, n, 16 * part:16 * part + 16, :].astype(jnp.float32) for g in range(8)], axis=0)
                out[bl, part] = tile.T


def local(gamma, rhs):
    vmem = pl.BlockSpec(memory_space=pltpu.VMEM)
    dma = pltpu.SemaphoreType.DMA
    f32, bf16 = jnp.float32, jnp.bfloat16
    shape = jax.ShapeDtypeStruct(rhs.shape, f32)
    gathered = pl.pallas_call(
        kernel,
        out_shape=jax.ShapeDtypeStruct((2, 8, 2, 32, T), bf16),
        in_specs=[pl.BlockSpec(memory_space=pl.ANY)] * 2,
        out_specs=vmem,
        scratch_shapes=[
            pltpu.VMEM((4, 4, 10, T, T), bf16),
            pltpu.VMEM((2, 2, T, T), f32),
            pltpu.VMEM((2, 8, 32, T), f32),
            pltpu.VMEM((16, 32, T), f32),
            pltpu.VMEM((ITERS, 2, 16, 32, T), bf16),
            pltpu.VMEM((16, 64, T), bf16),
            pltpu.VMEM((2, SB, 32, 256), f32),
            pltpu.VMEM((ITERS, SB, 32, 256), f32),
            pltpu.VMEM((2, 8, T), f32),
            pltpu.VMEM((32, N), f32),
            pltpu.VMEM((32, N), f32),
            pltpu.VMEM((32, N), f32),
            pltpu.VMEM((32, N), f32),
            pltpu.VMEM((16, 2, 32, T), bf16),
            pltpu.VMEM((2, 8, 2, 32, T), bf16),
            dma((10,)), dma((12,)), dma((10,)), dma((16,)), dma((16,)), dma((16, 6, 2)), dma((6, 4)), dma((6, 8)),
            dma((ITERS,)), dma((ITERS,)), dma((ITERS,)), dma((ITERS,)), dma((1,)), dma((1,)),
            dma((2, 8)), dma((16,)), dma((1,)),
        ],
        compiler_params=pltpu.CompilerParams(
            collective_id=0, has_side_effects=True, vmem_limit_bytes=60 * 2**20),
    )(gamma, rhs)
    return pl.pallas_call(turn_back, out_shape=(shape, shape), in_specs=[vmem], out_specs=(vmem, vmem))(gathered)


def solution(mesh):
    spec = P("bin", None, "row", "col")
    return jax.shard_map(local, mesh=mesh, in_specs=(spec, spec), out_specs=(spec, spec), check_vma=False)
```

```python
import jax
import jax.numpy as jnp
from jax import lax
from jax.experimental import pallas as pl
from jax.experimental.pallas import tpu as pltpu
from jax.sharding import PartitionSpec as P

MESH = pl.DeviceIdType.MESH
N = 2048
ITERS = 3
EPS_REL = 0.1
T = 128
SB = 8
FAR_FIRST = ((2, 2), (2, 1), (2, 3), (1, 2), (3, 2), (1, 1), (1, 3), (3, 1), (3, 3), (2, 0), (0, 2), (1, 0), (3, 0), (0, 1), (0, 3), (0, 0))
APART = (0, 3, 6, 1, 4)
CHUNKS = ((0, 2), (2, 4), (4, 6), (6, 8), (8, 9), (9, 10))


def kernel(gamma, rhs, out,
           W, tile_in, bT, B, X, Xs, Y, Z, shs, dir_, res, sol, img, O, R,
           zr, zs, ws, br, bs, rs, gs, ss, xr, xs, yr, ys, shr_sem, shs_sem, orr, ors, in_sem):
    h = lax.axis_index("bin")
    i = lax.axis_index("row")
    z = lax.axis_index("col")
    y, x = i // 4, i % 4
    hb, bl_me = (z % 4) // 2, z % 2
    big = i // 2
    home = (z + 17 + y % 2 - x) % 16

    fetch = pltpu.make_async_copy(rhs, tile_in, in_sem.at[0])
    fetch.start()

    def dev(b, r, c):
        return {"bin": b, "row": r, "col": c}

    def is_me(b, r, c):
        return (b == h) & (r == i) & (c == z)

    def step_x(row, d):
        return (row // 4) * 4 + (row % 4 + d) % 4

    def step_y(row, d):
        return (row // 4 + d) % 4 * 4 + row % 4

    def step_z(d):
        return (z + d + 16) % 16

    barrier = pltpu.get_barrier_semaphore()

    def greet(b, r, c, maybe_me):
        def far():
            pl.semaphore_signal(barrier, inc=1, device_id=dev(b, r, c), device_id_type=MESH)
        if maybe_me:
            pl.when(jnp.logical_not(is_me(b, r, c)))(far)
        else:
            far()

    for d in (4, -4):
        greet(hb, i, step_z(d), False)
        greet(h, i, step_z(d), False)
    for d in (3, -3, 2, -2, 1, -1):
        greet(hb, i, step_z(d), False)
    greet(hb, i, z, True)
    for k in range(16):
        greet(hb, k, home, True)
    for d in (1, 2, 3):
        greet(h, step_x(i, d), z, False)
        greet(h, step_y(i, d), z, False)
    greet(1 - h, i, z, False)

    mine = jnp.where(h == hb, 1, 0)
    pl.semaphore_wait(barrier, 33 + mine - mine * jnp.where(x == 1 + y % 2, 1, 0))

    def send(src, dst, send_sem, recv_sem, target):
        return pltpu.make_async_remote_copy(
            src_ref=src, dst_ref=dst, send_sem=send_sem, recv_sem=recv_sem,
            device_id=dev(*target), device_id_type=MESH)

    sib = (1 - h, i, z)

    apart = (z // 2 - big + 8) % 8
    slot = jnp.where(apart == 0, 0, jnp.where(apart == 3, 1, jnp.where(apart == 6, 2, jnp.where(apart == 1, 3, 4))))
    chosen = (slot < 4) | ((apart == 4) & (big < 4))
    t = 2 * slot + z % 2

    def tile_copies():
        n = 0
        for bl in range(2):
            ahead = (2 * h + bl + 4 - z % 4) % 4
            for q in range(2):
                for kind in range(3):
                    if kind == 0:
                        target, cond = (q, i, step_z(ahead)), jnp.logical_not((ahead == 0) & (q == h))
                    elif kind == 1:
                        target, cond = (q, i, step_z(ahead - 4)), True
                    else:
                        target, cond = (q, i, step_z(4)), ahead == 0
                    yield cond, target, gamma.at[bl, q], zs.at[n]
                    n += 1

    def when(cond, body):
        if cond is True:
            body()
        else:
            pl.when(cond)(body)

    def send_tiles():
        for cond, target, src, sem in tile_copies():
            when(cond, lambda: send(src, W.at[y, x, t], sem, zr.at[t], target).start())
        @pl.when(h == hb)
        def _():
            pltpu.make_async_copy(gamma.at[bl_me, h], W.at[y, x, t], zr.at[t]).start()

    def tile_wait(u):
        send(gamma.at[0, 0], W.at[y, x, u], zs.at[0], zr.at[u], sib).wait_recv()

    def route(u):
        off = (z - 2 * (big + APART[u // 2]) - u % 2 + 32) % 16
        up = ((off >= 1) & (off <= 3)) | ((off == 4) & (h == 0))
        down = (off >= 13) | ((off == 12) & (h == 1))
        near = (off <= 4) | (off >= 12)
        return near, up | down, (h, i, step_z(jnp.where(up, 4, -4)))

    def tile_pass(u, target):
        return send(W.at[y, x, u], W.at[y, x, u], ws.at[u], zr.at[u], target)

    def slot_ok(u, row):
        return True if u < 8 else row < 8

    def both_conds(a, b):
        return a if b is True else a & b

    def near_tiles(slots):
        for u in slots:
            near, relay, target = route(u)
            @pl.when(both_conds(near, slot_ok(u, i)))
            def _(u=u, relay=relay, target=target):
                tile_wait(u)
                @pl.when(relay)
                def _():
                    tile_pass(u, target).start()

    def far_tiles(slots):
        for u in slots:
            near, _, _ = route(u)
            @pl.when(both_conds(jnp.logical_not(near), slot_ok(u, i)))
            def _(u=u):
                tile_wait(u)

    def turn_rhs():
        fetch.wait()
        for bl in range(2):
            for part in range(2):
                tile = tile_in[bl, part].T
                for g in range(8):
                    bT[bl, g, 16 * part:16 * part + 16, :] = tile[16 * g:16 * g + 16, :]

    def rhs_copies():
        n = 0
        for bl in range(2):
            for yy in range(4):
                xx = (2 * h + bl + 5 + yy % 2 - z % 4) % 4
                for q in range(2):
                    target = (q, 4 * yy + xx, (z + 15 - yy % 2 + xx) % 16)
                    yield is_me(*target), target, bT.at[bl, 2 * yy + q], bs.at[n]
                    n += 1

    def send_rhs():
        for me, target, src, sem in rhs_copies():
            pl.when(jnp.logical_not(me))(lambda: send(src, B.at[i], sem, br.at[i], target).start())
            pl.when(me)(lambda: pltpu.make_async_copy(src, B.at[i], br.at[i]).start())

    def panel_send(row, c, n, target_row):
        a, b = CHUNKS[c]
        ref = W.at[row // 4, row % 4, a:b]
        return send(ref, ref, ss.at[c, n], rs.at[row, c], (h, target_row, z))

    def group_send(line, c, n, part, sem, target_row):
        a, b = CHUNKS[c]
        size = 2 if c == 5 else 4
        lo, hi = (0, size) if part is None else (part * size // 2, (part + 1) * size // 2)
        ref = W.at[line, lo:hi, a:b] if c % 2 == 0 else W.at[lo:hi, line, a:b]
        return send(ref, ref, ss.at[c, n], gs.at[c, sem], (h, target_row, z))

    def axes(c):
        return (step_x, step_y) if c % 2 == 0 else (step_y, step_x)

    def line_of(c, row):
        return row // 4 if c % 2 == 0 else row % 4

    def row_ok(c, row):
        return True if c < 4 else row < 8

    def line_ok(c, line):
        return line < 2 if c == 4 else True

    def stage_a(c):
        first, _ = axes(c)
        def body():
            for n, e in enumerate((1, 3, 2)):
                panel_send(i, c, n, first(i, e)).start()
        when(row_ok(c, i), body)

    def stage_b(c):
        first, second = axes(c)
        for e in (1, 3, 2):
            row = first(i, e)
            when(row_ok(c, row), lambda: panel_send(row, c, 0, first(i, 1)).wait_recv())
        line = line_of(c, i)
        def body():
            group_send(line, c, 3, None, 1, second(i, 1)).start()
            group_send(line, c, 4, None, 0, second(i, 3)).start()
        when(line_ok(c, line), body)

    def stage_c(c):
        _, second = axes(c)
        for side, part in ((1, 0), (3, 1)):
            line = line_of(c, second(i, side))
            def body():
                group_send(line, c, 3, None, part, second(i, 1)).wait_recv()
                group_send(line, c, 5 + part, part, 2 + part, second(i, 4 - side)).start()
            when(line_ok(c, line), body)

    def stage_e(c):
        _, second = axes(c)
        line = line_of(c, second(i, 2))
        def body():
            for part in range(2):
                group_send(line, c, 3, part, 2 + part, second(i, 1)).wait_recv()
        when(line_ok(c, line), body)

    def x_copy(it):
        return send(X.at[it, h], X.at[it, h], xs.at[it], xr.at[it], sib)

    sign = jnp.where(h == 0, 1.0, -1.0).astype(jnp.bfloat16)

    def x_ready(it):
        x_copy(it).wait_recv()
        for k in range(16):
            Xs[k] = X[it, :, k].reshape(64, T) * sign

    def rhs_arrived():
        for k in range(16):
            send(bT.at[0, 0], B.at[k], bs.at[0], br.at[k], sib).wait_recv()
            X[0, h, k] = B[k].astype(jnp.bfloat16)
        x_copy(0).start()
        for k in range(16):
            cols = slice(T * k, T * k + T)
            dir_[:, cols] = B[k]
            res[:, cols] = B[k]
        sol[...] = jnp.zeros_like(sol)

    def super_tile(a, n):
        return jnp.concatenate(
            [jnp.concatenate([W[a // 2, r, 2 * n], W[a // 2, r, 2 * n + 1]], axis=1)
             for r in (2 * (a % 2), 2 * (a % 2) + 1)], axis=0)

    def products(it, c, n, acc):
        def add(acc, v):
            return v if acc is None else acc + v
        d = APART[n]
        a = (c - d) % SB
        if n < 4 or a < 4:
            left = jnp.concatenate([Xs[2 * a], Xs[2 * a + 1]], axis=1)
            acc = add(acc, jnp.dot(left, super_tile(a, n), preferred_element_type=jnp.float32))
        k = (c + d) % SB
        if n > 0 and (n < 4 or c < 4):
            left = jnp.concatenate([X[it, :, 2 * k].reshape(64, T), X[it, :, 2 * k + 1].reshape(64, T)], axis=1)
            acc = add(acc, lax.dot_general(
                left, super_tile(c, n), (((1,), (1,)), ((), ())), preferred_element_type=jnp.float32))
        return acc

    def y_copy(it):
        return send(Y.at[1 - h], Z.at[it], ys.at[it], yr.at[it], sib)

    def first_product(n):
        for c in range(SB):
            acc = products(0, c, n, None if n == 0 else Y[:, c].reshape(64, 256))
            Y[:, c] = acc.reshape(2, 32, 256)

    pl.when(chosen)(send_tiles)
    turn_rhs()
    send_rhs()
    near_tiles(range(10))
    for c in range(6):
        far_tiles(range(*CHUNKS[c]))
        stage_a(c)
    rhs_arrived()
    for c in range(6):
        stage_b(c)
    for c in range(6):
        stage_c(c)
    x_ready(0)
    for c in range(4):
        stage_e(c)
        first_product(c)
    stage_e(4)
    stage_e(5)
    first_product(4)
    y_copy(0).start()

    total = jnp.zeros((T, T), jnp.float32)
    for k in range(16):
        total = total + W[k // 4, k % 4, k % 2].astype(jnp.float32)
    eye = lax.broadcasted_iota(jnp.int32, (T, T), 0) == lax.broadcasted_iota(jnp.int32, (T, T), 1)
    total = jnp.where(eye, total, 0.0)
    trace = jnp.sum(jnp.sum(total, axis=0, keepdims=True), axis=1, keepdims=True)
    shs[0] = jnp.broadcast_to(EPS_REL * trace / N, (8, T))
    shift_copy = send(shs.at[0], shs.at[1], shs_sem.at[0], shr_sem.at[0], sib)
    shift_copy.start()

    def both(v):
        s = v[:16] + v[16:]
        return jnp.concatenate([s, s], axis=0)

    def row_sum(parts):
        total = parts[0]
        for p in parts[1:]:
            total = total + p
        return both(jnp.sum(total, axis=1, keepdims=True))

    slabs = [slice(256 * c, 256 * c + 256) for c in range(SB)]
    rr0 = row_sum([res[:, s] * res[:, s] for s in slabs])
    shift_copy.wait()
    shift = jnp.where(h == 0, shs[0], shs[1])[:1, :1]

    def iteration(it, rr):
        y_copy(it).wait()
        curve = []
        for c, s in enumerate(slabs):
            own, other = Y[h, c], Z[it, c]
            real = jnp.where(h == 0, own, other)
            imag = jnp.where(h == 0, other, own)
            d = dir_[:, s]
            image = real + jnp.concatenate([-imag[16:], imag[:16]], axis=0) + shift * d
            img[:, s] = image
            curve.append(d * image)
        alpha = rr / row_sum(curve)
        norm = []
        for s in slabs:
            sol[:, s] = sol[:, s] + alpha * dir_[:, s]
            r = res[:, s] - alpha * img[:, s]
            res[:, s] = r
            norm.append(r * r)
        new = row_sum(norm)

        @pl.when(it + 1 < ITERS)
        def _():
            beta = new / rr
            for k in range(16):
                cols = slice(T * k, T * k + T)
                d = res[:, cols] + beta * dir_[:, cols]
                dir_[:, cols] = d
                X[it + 1, h, k] = d.astype(jnp.bfloat16)
            x_copy(it + 1).start()
            x_ready(it + 1)
            for c in range(SB):
                acc = None
                for n in range(5):
                    acc = products(it + 1, c, n, acc)
                Y[:, c] = acc.reshape(2, 32, 256)
            y_copy(it + 1).start()

        return new

    lax.fori_loop(0, ITERS, iteration, rr0)

    dst, arrive = R.at[bl_me, 2 * y + h], orr.at[bl_me, 2 * y + h]

    def out_copies():
        for n, (dy, dx) in enumerate(FAR_FIRST):
            row = step_y(step_x(i, dx), dy)
            target = (hb, row, home)
            yield (is_me(*target) if dx + dy == 0 else None), target, O.at[row], ors.at[n]

    for k in range(16):
        cols = slice(T * k, T * k + T)
        O[k, 0] = sol[:, cols].astype(jnp.bfloat16)
        O[k, 1] = res[:, cols].astype(jnp.bfloat16)
    for me, target, src, sem in out_copies():
        go = lambda: send(src, dst, sem, arrive, target).start()
        if me is None:
            go()
        else:
            pl.when(jnp.logical_not(me))(go)
            pl.when(me)(lambda: pltpu.make_async_copy(src, dst, arrive).start())

    @pl.when(chosen)
    def _():
        for cond, target, src, sem in tile_copies():
            when(cond, lambda: send(src, W.at[y, x, t], sem, zr.at[t], target).wait_send())
    for u in range(10):
        _, relay, target = route(u)
        pl.when(both_conds(relay, slot_ok(u, i)))(lambda: tile_pass(u, target).wait_send())
    for me, target, src, sem in rhs_copies():
        pl.when(jnp.logical_not(me))(lambda: send(src, B.at[i], sem, br.at[i], target).wait_send())
    for c in range(6):
        _, second = axes(c)
        def own():
            for n in range(3):
                panel_send(i, c, n, step_x(i, 1)).wait_send()
        when(row_ok(c, i), own)
        line = line_of(c, i)
        def group():
            for n in (3, 4):
                group_send(line, c, n, None, 0, step_x(i, 1)).wait_send()
        when(line_ok(c, line), group)
        for side, part in ((1, 0), (3, 1)):
            line = line_of(c, second(i, side))
            when(line_ok(c, line), lambda: group_send(line, c, 5 + part, part, 0, step_x(i, 1)).wait_send())
    for it in range(ITERS):
        x_copy(it).wait_send()

    for bl in range(2):
        for g in range(8):
            send(O.at[0], R.at[bl, g], ors.at[0], orr.at[bl, g], sib).wait_recv()
    out[...] = R[...]
    for me, target, src, sem in out_copies():
        when(True if me is None else jnp.logical_not(me), lambda: send(src, dst, sem, arrive, target).wait_send())


def turn_back(r, out_s, out_r):
    for bl in range(2):
        for n, out in enumerate((out_s, out_r)):
            for part in range(2):
                tile = jnp.concatenate(
                    [r[bl, g, n, 16 * part:16 * part + 16, :].astype(jnp.float32) for g in range(8)], axis=0)
                out[bl, part] = tile.T


def local(gamma, rhs):
    vmem = pl.BlockSpec(memory_space=pltpu.VMEM)
    dma = pltpu.SemaphoreType.DMA
    f32, bf16 = jnp.float32, jnp.bfloat16
    shape = jax.ShapeDtypeStruct(rhs.shape, f32)
    gathered = pl.pallas_call(
        kernel,
        out_shape=jax.ShapeDtypeStruct((2, 8, 2, 32, T), bf16),
        in_specs=[pl.BlockSpec(memory_space=pl.ANY)] * 2,
        out_specs=vmem,
        scratch_shapes=[
            pltpu.VMEM((4, 4, 10, T, T), bf16),
            pltpu.VMEM((2, 2, T, T), f32),
            pltpu.VMEM((2, 8, 32, T), f32),
            pltpu.VMEM((16, 32, T), f32),
            pltpu.VMEM((ITERS, 2, 16, 32, T), bf16),
            pltpu.VMEM((16, 64, T), bf16),
            pltpu.VMEM((2, SB, 32, 256), f32),
            pltpu.VMEM((ITERS, SB, 32, 256), f32),
            pltpu.VMEM((2, 8, T), f32),
            pltpu.VMEM((32, N), f32),
            pltpu.VMEM((32, N), f32),
            pltpu.VMEM((32, N), f32),
            pltpu.VMEM((32, N), f32),
            pltpu.VMEM((16, 2, 32, T), bf16),
            pltpu.VMEM((2, 8, 2, 32, T), bf16),
            dma((10,)), dma((12,)), dma((10,)), dma((16,)), dma((16,)), dma((16, 6)), dma((6, 4)), dma((6, 7)),
            dma((ITERS,)), dma((ITERS,)), dma((ITERS,)), dma((ITERS,)), dma((1,)), dma((1,)),
            dma((2, 8)), dma((16,)), dma((1,)),
        ],
        compiler_params=pltpu.CompilerParams(
            collective_id=0, has_side_effects=True, vmem_limit_bytes=60 * 2**20),
    )(gamma, rhs)
    return pl.pallas_call(turn_back, out_shape=(shape, shape), in_specs=[vmem], out_specs=(vmem, vmem))(gathered)


def solution(mesh):
    spec = P("bin", None, "row", "col")
    return jax.shard_map(local, mesh=mesh, in_specs=(spec, spec), out_specs=(spec, spec), check_vma=False)
```

```python
import jax
import jax.numpy as jnp
from jax import lax
from jax.experimental import pallas as pl
from jax.experimental.pallas import tpu as pltpu
from jax.sharding import PartitionSpec as P

MESH = pl.DeviceIdType.MESH
N = 2048
ITERS = 3
EPS_REL = 0.1
T = 128
SB = 8
FAR_FIRST = ((2, 2), (2, 1), (2, 3), (1, 2), (3, 2), (1, 1), (1, 3), (3, 1), (3, 3), (2, 0), (0, 2), (1, 0), (3, 0), (0, 1), (0, 3), (0, 0))
APART = (0, 3, 6, 1, 4)
CHUNKS = ((0, 2), (2, 4), (4, 6), (6, 8), (8, 9), (9, 10))


def kernel(gamma, rhs, out,
           W, tile_in, bT, B, X, Xs, Y, Z, shs, dir_, res, sol, img, O, R,
           zr, zs, ws, br, bs, rs, gs, ss, xr, xs, yr, ys, shr_sem, shs_sem, orr, ors, in_sem):
    h = lax.axis_index("bin")
    i = lax.axis_index("row")
    z = lax.axis_index("col")
    y, x = i // 4, i % 4
    hb, bl_me = (z % 4) // 2, z % 2
    big = i // 2
    home = (z + 17 + y % 2 - x) % 16

    fetch = pltpu.make_async_copy(rhs, tile_in, in_sem.at[0])
    fetch.start()

    def dev(b, r, c):
        return {"bin": b, "row": r, "col": c}

    def is_me(b, r, c):
        return (b == h) & (r == i) & (c == z)

    def step_x(row, d):
        return (row // 4) * 4 + (row % 4 + d) % 4

    def step_y(row, d):
        return (row // 4 + d) % 4 * 4 + row % 4

    def step_z(d):
        return (z + d + 16) % 16

    barrier = pltpu.get_barrier_semaphore()

    def greet(b, r, c, maybe_me):
        def far():
            pl.semaphore_signal(barrier, inc=1, device_id=dev(b, r, c), device_id_type=MESH)
        if maybe_me:
            pl.when(jnp.logical_not(is_me(b, r, c)))(far)
        else:
            far()

    for d in (4, -4):
        greet(hb, i, step_z(d), False)
        greet(h, i, step_z(d), False)
    for d in (3, -3, 2, -2, 1, -1):
        greet(hb, i, step_z(d), False)
    greet(hb, i, z, True)
    for k in range(16):
        greet(hb, k, home, True)
    for d in (1, 2, 3):
        greet(h, step_x(i, d), z, False)
        greet(h, step_y(i, d), z, False)
    greet(1 - h, i, z, False)

    mine = jnp.where(h == hb, 1, 0)
    pl.semaphore_wait(barrier, 33 + mine - mine * jnp.where(x == 1 + y % 2, 1, 0))

    def send(src, dst, send_sem, recv_sem, target):
        return pltpu.make_async_remote_copy(
            src_ref=src, dst_ref=dst, send_sem=send_sem, recv_sem=recv_sem,
            device_id=dev(*target), device_id_type=MESH)

    sib = (1 - h, i, z)

    apart = (z // 2 - big + 8) % 8
    slot = jnp.where(apart == 0, 0, jnp.where(apart == 3, 1, jnp.where(apart == 6, 2, jnp.where(apart == 1, 3, 4))))
    chosen = (slot < 4) | ((apart == 4) & (big < 4))
    t = 2 * slot + z % 2

    def tile_copies():
        n = 0
        for bl in range(2):
            ahead = (2 * h + bl + 4 - z % 4) % 4
            for q in range(2):
                for kind in range(3):
                    if kind == 0:
                        target, cond = (q, i, step_z(ahead)), jnp.logical_not((ahead == 0) & (q == h))
                    elif kind == 1:
                        target, cond = (q, i, step_z(ahead - 4)), True
                    else:
                        target, cond = (q, i, step_z(4)), ahead == 0
                    yield cond, target, gamma.at[bl, q], zs.at[n]
                    n += 1

    def when(cond, body):
        if cond is True:
            body()
        else:
            pl.when(cond)(body)

    def send_tiles():
        for cond, target, src, sem in tile_copies():
            when(cond, lambda: send(src, W.at[y, x, t], sem, zr.at[t], target).start())
        @pl.when(h == hb)
        def _():
            pltpu.make_async_copy(gamma.at[bl_me, h], W.at[y, x, t], zr.at[t]).start()

    def tile_wait(u):
        send(gamma.at[0, 0], W.at[y, x, u], zs.at[0], zr.at[u], sib).wait_recv()

    def route(u):
        off = (z - 2 * (big + APART[u // 2]) - u % 2 + 32) % 16
        up = ((off >= 1) & (off <= 3)) | ((off == 4) & (h == 0))
        down = (off >= 13) | ((off == 12) & (h == 1))
        near = (off <= 4) | (off >= 12)
        return near, up | down, (h, i, step_z(jnp.where(up, 4, -4)))

    def tile_pass(u, target):
        return send(W.at[y, x, u], W.at[y, x, u], ws.at[u], zr.at[u], target)

    def slot_ok(u, row):
        return True if u < 8 else row < 8

    def both_conds(a, b):
        return a if b is True else a & b

    def near_tiles(slots):
        for u in slots:
            near, relay, target = route(u)
            @pl.when(both_conds(near, slot_ok(u, i)))
            def _(u=u, relay=relay, target=target):
                tile_wait(u)
                @pl.when(relay)
                def _():
                    tile_pass(u, target).start()

    def far_tiles(slots):
        for u in slots:
            near, _, _ = route(u)
            @pl.when(both_conds(jnp.logical_not(near), slot_ok(u, i)))
            def _(u=u):
                tile_wait(u)

    def turn_rhs():
        fetch.wait()
        for bl in range(2):
            for part in range(2):
                tile = tile_in[bl, part].T
                for g in range(8):
                    bT[bl, g, 16 * part:16 * part + 16, :] = tile[16 * g:16 * g + 16, :]

    def rhs_copies():
        n = 0
        for bl in range(2):
            for yy in range(4):
                xx = (2 * h + bl + 5 + yy % 2 - z % 4) % 4
                for q in range(2):
                    target = (q, 4 * yy + xx, (z + 15 - yy % 2 + xx) % 16)
                    yield is_me(*target), target, bT.at[bl, 2 * yy + q], bs.at[n]
                    n += 1

    def send_rhs():
        for me, target, src, sem in rhs_copies():
            pl.when(jnp.logical_not(me))(lambda: send(src, B.at[i], sem, br.at[i], target).start())
            pl.when(me)(lambda: pltpu.make_async_copy(src, B.at[i], br.at[i]).start())

    def panel_send(row, c, n, target_row):
        a, b = CHUNKS[c]
        ref = W.at[row // 4, row % 4, a:b]
        return send(ref, ref, ss.at[c, n], rs.at[row, c], (h, target_row, z))

    def group_send(line, c, n, part, sem, target_row):
        a, b = CHUNKS[c]
        size = 2 if c == 5 else 4
        lo, hi = (0, size) if part is None else (part * size // 2, (part + 1) * size // 2)
        ref = W.at[line, lo:hi, a:b] if c % 2 == 0 else W.at[lo:hi, line, a:b]
        return send(ref, ref, ss.at[c, n], gs.at[c, sem], (h, target_row, z))

    def axes(c):
        return (step_x, step_y) if c % 2 == 0 else (step_y, step_x)

    def line_of(c, row):
        return row // 4 if c % 2 == 0 else row % 4

    def row_ok(c, row):
        return True if c < 4 else row < 8

    def line_ok(c, line):
        return line < 2 if c == 4 else True

    def stage_a(c):
        first, _ = axes(c)
        def body():
            for n, e in enumerate((1, 3, 2)):
                panel_send(i, c, n, first(i, e)).start()
        when(row_ok(c, i), body)

    def stage_b(c):
        first, second = axes(c)
        for e in (1, 3, 2):
            row = first(i, e)
            when(row_ok(c, row), lambda: panel_send(row, c, 0, first(i, 1)).wait_recv())
        line = line_of(c, i)
        def body():
            group_send(line, c, 3, None, 1, second(i, 1)).start()
            group_send(line, c, 4, None, 0, second(i, 3)).start()
        when(line_ok(c, line), body)

    def stage_c(c):
        _, second = axes(c)
        for side, part in ((1, 0), (3, 1)):
            line = line_of(c, second(i, side))
            def body():
                group_send(line, c, 3, None, part, second(i, 1)).wait_recv()
                group_send(line, c, 5 + part, part, 2 + part, second(i, 4 - side)).start()
            when(line_ok(c, line), body)

    def stage_e(c):
        _, second = axes(c)
        line = line_of(c, second(i, 2))
        def body():
            for part in range(2):
                group_send(line, c, 3, part, 2 + part, second(i, 1)).wait_recv()
        when(line_ok(c, line), body)

    def x_copy(it):
        return send(X.at[it, h], X.at[it, h], xs.at[it], xr.at[it], sib)

    sign = jnp.where(h == 0, 1.0, -1.0).astype(jnp.bfloat16)

    def x_ready(it):
        x_copy(it).wait_recv()
        for k in range(16):
            Xs[k] = X[it, :, k].reshape(64, T) * sign

    def rhs_arrived():
        for k in range(16):
            send(bT.at[0, 0], B.at[k], bs.at[0], br.at[k], sib).wait_recv()
            X[0, h, k] = B[k].astype(jnp.bfloat16)
        x_copy(0).start()
        for k in range(16):
            cols = slice(T * k, T * k + T)
            dir_[:, cols] = B[k]
            res[:, cols] = B[k]
        sol[...] = jnp.zeros_like(sol)

    def super_tile(a, n):
        return jnp.concatenate(
            [jnp.concatenate([W[a // 2, r, 2 * n], W[a // 2, r, 2 * n + 1]], axis=1)
             for r in (2 * (a % 2), 2 * (a % 2) + 1)], axis=0)

    def products(it, c, n, acc):
        def add(acc, v):
            return v if acc is None else acc + v
        d = APART[n]
        a = (c - d) % SB
        if n < 4 or a < 4:
            left = jnp.concatenate([Xs[2 * a], Xs[2 * a + 1]], axis=1)
            acc = add(acc, jnp.dot(left, super_tile(a, n), preferred_element_type=jnp.float32))
        k = (c + d) % SB
        if n > 0 and (n < 4 or c < 4):
            left = jnp.concatenate([X[it, :, 2 * k].reshape(64, T), X[it, :, 2 * k + 1].reshape(64, T)], axis=1)
            acc = add(acc, lax.dot_general(
                left, super_tile(c, n), (((1,), (1,)), ((), ())), preferred_element_type=jnp.float32))
        return acc

    def y_copy(it):
        return send(Y.at[1 - h], Z.at[it], ys.at[it], yr.at[it], sib)

    def first_product(n):
        for c in range(SB):
            acc = products(0, c, n, None if n == 0 else Y[:, c].reshape(64, 256))
            Y[:, c] = acc.reshape(2, 32, 256)

    pl.when(chosen)(send_tiles)
    turn_rhs()
    send_rhs()
    near_tiles(range(10))
    for c in range(6):
        far_tiles(range(*CHUNKS[c]))
        stage_a(c)
    rhs_arrived()
    for c in range(6):
        stage_b(c)
    for c in range(6):
        stage_c(c)
    x_ready(0)
    for c in range(4):
        stage_e(c)
        first_product(c)
    total = jnp.zeros((T, T), jnp.float32)
    for k in range(16):
        total = total + W[k // 4, k % 4, k % 2].astype(jnp.float32)
    eye = lax.broadcasted_iota(jnp.int32, (T, T), 0) == lax.broadcasted_iota(jnp.int32, (T, T), 1)
    total = jnp.where(eye, total, 0.0)
    trace = jnp.sum(jnp.sum(total, axis=0, keepdims=True), axis=1, keepdims=True)
    shs[0] = jnp.broadcast_to(EPS_REL * trace / N, (8, T))
    shift_copy = send(shs.at[0], shs.at[1], shs_sem.at[0], shr_sem.at[0], sib)
    shift_copy.start()

    stage_e(4)
    stage_e(5)
    first_product(4)
    y_copy(0).start()

    def both(v):
        s = v[:16] + v[16:]
        return jnp.concatenate([s, s], axis=0)

    def row_sum(parts):
        total = parts[0]
        for p in parts[1:]:
            total = total + p
        return both(jnp.sum(total, axis=1, keepdims=True))

    slabs = [slice(256 * c, 256 * c + 256) for c in range(SB)]
    rr0 = row_sum([res[:, s] * res[:, s] for s in slabs])
    shift_copy.wait()
    shift = jnp.where(h == 0, shs[0], shs[1])[:1, :1]

    def iteration(it, rr):
        y_copy(it).wait()
        curve = []
        for c, s in enumerate(slabs):
            own, other = Y[h, c], Z[it, c]
            real = jnp.where(h == 0, own, other)
            imag = jnp.where(h == 0, other, own)
            d = dir_[:, s]
            image = real + jnp.concatenate([-imag[16:], imag[:16]], axis=0) + shift * d
            img[:, s] = image
            curve.append(d * image)
        alpha = rr / row_sum(curve)
        norm = []
        for s in slabs:
            sol[:, s] = sol[:, s] + alpha * dir_[:, s]
            r = res[:, s] - alpha * img[:, s]
            res[:, s] = r
            norm.append(r * r)
        new = row_sum(norm)

        @pl.when(it + 1 < ITERS)
        def _():
            beta = new / rr
            for k in range(16):
                cols = slice(T * k, T * k + T)
                d = res[:, cols] + beta * dir_[:, cols]
                dir_[:, cols] = d
                X[it + 1, h, k] = d.astype(jnp.bfloat16)
            x_copy(it + 1).start()
            x_ready(it + 1)
            for c in range(SB):
                acc = None
                for n in range(5):
                    acc = products(it + 1, c, n, acc)
                Y[:, c] = acc.reshape(2, 32, 256)
            y_copy(it + 1).start()

        return new

    lax.fori_loop(0, ITERS, iteration, rr0)

    dst, arrive = R.at[bl_me, 2 * y + h], orr.at[bl_me, 2 * y + h]

    def out_copies():
        for n, (dy, dx) in enumerate(FAR_FIRST):
            row = step_y(step_x(i, dx), dy)
            target = (hb, row, home)
            yield (is_me(*target) if dx + dy == 0 else None), target, O.at[row], ors.at[n]

    for k in range(16):
        cols = slice(T * k, T * k + T)
        O[k, 0] = sol[:, cols].astype(jnp.bfloat16)
        O[k, 1] = res[:, cols].astype(jnp.bfloat16)
    for me, target, src, sem in out_copies():
        go = lambda: send(src, dst, sem, arrive, target).start()
        if me is None:
            go()
        else:
            pl.when(jnp.logical_not(me))(go)
            pl.when(me)(lambda: pltpu.make_async_copy(src, dst, arrive).start())

    @pl.when(chosen)
    def _():
        for cond, target, src, sem in tile_copies():
            when(cond, lambda: send(src, W.at[y, x, t], sem, zr.at[t], target).wait_send())
    for u in range(10):
        _, relay, target = route(u)
        pl.when(both_conds(relay, slot_ok(u, i)))(lambda: tile_pass(u, target).wait_send())
    for me, target, src, sem in rhs_copies():
        pl.when(jnp.logical_not(me))(lambda: send(src, B.at[i], sem, br.at[i], target).wait_send())
    for c in range(6):
        _, second = axes(c)
        def own():
            for n in range(3):
                panel_send(i, c, n, step_x(i, 1)).wait_send()
        when(row_ok(c, i), own)
        line = line_of(c, i)
        def group():
            for n in (3, 4):
                group_send(line, c, n, None, 0, step_x(i, 1)).wait_send()
        when(line_ok(c, line), group)
        for side, part in ((1, 0), (3, 1)):
            line = line_of(c, second(i, side))
            when(line_ok(c, line), lambda: group_send(line, c, 5 + part, part, 0, step_x(i, 1)).wait_send())
    for it in range(ITERS):
        x_copy(it).wait_send()

    for bl in range(2):
        for g in range(8):
            send(O.at[0], R.at[bl, g], ors.at[0], orr.at[bl, g], sib).wait_recv()
    out[...] = R[...]
    for me, target, src, sem in out_copies():
        when(True if me is None else jnp.logical_not(me), lambda: send(src, dst, sem, arrive, target).wait_send())


def turn_back(r, out_s, out_r):
    for bl in range(2):
        for n, out in enumerate((out_s, out_r)):
            for part in range(2):
                tile = jnp.concatenate(
                    [r[bl, g, n, 16 * part:16 * part + 16, :].astype(jnp.float32) for g in range(8)], axis=0)
                out[bl, part] = tile.T


def local(gamma, rhs):
    vmem = pl.BlockSpec(memory_space=pltpu.VMEM)
    dma = pltpu.SemaphoreType.DMA
    f32, bf16 = jnp.float32, jnp.bfloat16
    shape = jax.ShapeDtypeStruct(rhs.shape, f32)
    gathered = pl.pallas_call(
        kernel,
        out_shape=jax.ShapeDtypeStruct((2, 8, 2, 32, T), bf16),
        in_specs=[pl.BlockSpec(memory_space=pl.ANY)] * 2,
        out_specs=vmem,
        scratch_shapes=[
            pltpu.VMEM((4, 4, 10, T, T), bf16),
            pltpu.VMEM((2, 2, T, T), f32),
            pltpu.VMEM((2, 8, 32, T), f32),
            pltpu.VMEM((16, 32, T), f32),
            pltpu.VMEM((ITERS, 2, 16, 32, T), bf16),
            pltpu.VMEM((16, 64, T), bf16),
            pltpu.VMEM((2, SB, 32, 256), f32),
            pltpu.VMEM((ITERS, SB, 32, 256), f32),
            pltpu.VMEM((2, 8, T), f32),
            pltpu.VMEM((32, N), f32),
            pltpu.VMEM((32, N), f32),
            pltpu.VMEM((32, N), f32),
            pltpu.VMEM((32, N), f32),
            pltpu.VMEM((16, 2, 32, T), bf16),
            pltpu.VMEM((2, 8, 2, 32, T), bf16),
            dma((10,)), dma((12,)), dma((10,)), dma((16,)), dma((16,)), dma((16, 6)), dma((6, 4)), dma((6, 7)),
            dma((ITERS,)), dma((ITERS,)), dma((ITERS,)), dma((ITERS,)), dma((1,)), dma((1,)),
            dma((2, 8)), dma((16,)), dma((1,)),
        ],
        compiler_params=pltpu.CompilerParams(
            collective_id=0, has_side_effects=True, vmem_limit_bytes=60 * 2**20),
    )(gamma, rhs)
    return pl.pallas_call(turn_back, out_shape=(shape, shape), in_specs=[vmem], out_specs=(vmem, vmem))(gathered)


def solution(mesh):
    spec = P("bin", None, "row", "col")
    return jax.shard_map(local, mesh=mesh, in_specs=(spec, spec), out_specs=(spec, spec), check_vma=False)
```
